512 devices in a mesh: cd: 128 (over x, z, core), ij: 4 (over y).
Axes of the slice: x: 4, y: 4, z: 16, core: 2. Of those that a mesh axis runs over, the one named last changes fastest.
Arguments:
- amplitudes: bfloat16 [4, 512, 32768], P('ij', 'cd'), may hold values from -6 to 6
- integrals: bfloat16 [1152, 32768], P(None, 'cd'), may hold values from -0.25 to 0.25
- pair_irrep: int32 [4, 512], P('ij'), may hold values from 0 to 7
- cd_irrep: int32 [32768], P('cd'), may hold values from 0 to 7
- ab_irrep: int32 [1152], P('cd'), may hold values from 0 to 7
Outputs:
- ladder: bfloat16 [4, 512, 1152], P('ij', None, 'cd')
The draws below stay inside these ranges and needn't reach their ends.
All inputs are finite; a program needn't handle non-finite values.
Results may differ from the reference program's by a relative error of at most 0.0035.
Values may be sent and summed in bfloat16 or wider, within the bound.
No kernel may reach another device: no remote copies, remote signals or barrier semaphores. Data moves between devices by JAX's collectives and lax.ppermute only.
A program may use at most 64 MiB of HBM per device.

```python
import jax
import jax.numpy as jnp
from jax import lax

AB = 1152
IRREPS = 8
PAIR_ROWS = 512
CDS = 32768
N_IJ = 4


def leading_irrep(key):
    return jax.random.randint(jax.random.fold_in(key, 97), (), 0, IRREPS)


def spread_labels(key, leading, shape):
    share_key, roll_key, other_key = jax.random.split(key, 3)
    share = jax.random.randint(share_key, (), 80, 100)
    roll = jax.random.randint(roll_key, shape, 0, 100)
    others = jax.random.randint(other_key, shape, 0, IRREPS)
    return jnp.where(roll < share, leading, others).astype(jnp.int32)


def draw_pair_irrep(key, part):
    leading = leading_irrep(key)
    key = jax.random.fold_in(key, 11)
    return spread_labels(key, leading, (N_IJ, PAIR_ROWS))


def draw_cd_irrep(key, part):
    leading = leading_irrep(key)
    key = jax.random.fold_in(key, 23)
    return spread_labels(key, leading, (CDS,))


def draw_ab_irrep(key, part):
    leading = leading_irrep(key)
    key = jax.random.fold_in(key, 37)
    return spread_labels(key, leading, (AB,))


def spiked(entries, rng, source, target, blocks, factor):
    owner, partner = [(jnp.arange(entries.shape[dim]) // (entries.shape[dim] // blocks)).reshape([-1 if axis == dim else 1 for axis in range(entries.ndim)]) for dim in (source, target)]
    chosen = jax.random.permutation(rng, blocks)[partner]
    strong = (owner == chosen) | (owner == (partner + blocks // 2) % blocks)
    return jnp.where(strong, factor * entries, entries)


def block_levels(own_key, extent, cuts, smallest, top_value):
    level = 1.0
    for dim, blocks in cuts:
        heights = jax.random.uniform(jax.random.fold_in(jax.random.fold_in(own_key, 6), dim), (blocks,), jnp.float32, smallest / len(cuts), top_value / len(cuts))
        level = level * jnp.repeat(jnp.exp(heights), extent[dim] // blocks).reshape((-1,) + (1,) * (len(extent) - 1 - dim))
    return level


def centred(stream_key, extent, spread, limit, cuts=(), kind=jnp.bfloat16):
    entries = spread * jax.random.normal(stream_key, extent, jnp.float32)
    if cuts:
        entries = entries * block_levels(stream_key, extent, cuts, -0.22, 0.18)
    return jnp.clip(entries, -limit, limit).astype(kind)


def heavy_noise(stream_key, dims, scale, limit, shards, heavy, held_as=jnp.bfloat16):
    result = scale * jax.random.normal(stream_key, dims, jnp.float32)
    if shards:
        result = result * block_levels(stream_key, dims, shards, -0.22, 0.18)
    return jnp.clip(spiked(result, jax.random.fold_in(stream_key, 3), *heavy), -limit, limit).astype(held_as)


def setup_inputs(seed: int = 0) -> dict:
    splits = jax.random.split(jax.random.key(seed), 6)
    amplitudes = centred(splits[0], (N_IJ, PAIR_ROWS, CDS), 1.0, 6.0, ((0, 4), (1, 128)))
    integrals = heavy_noise(splits[1], (AB, CDS), (CDS // 4) ** -0.5, 0.25, ((1, 128),), (1, 0, 128, 5.5))
    pair_irrep = draw_pair_irrep(jax.random.fold_in(splits[5], 71), 0)
    cd_irrep = draw_cd_irrep(jax.random.fold_in(splits[5], 71), 0)
    ab_irrep = draw_ab_irrep(jax.random.fold_in(splits[5], 71), 0)
    return dict(amplitudes=amplitudes, integrals=integrals, pair_irrep=pair_irrep, cd_irrep=cd_irrep, ab_irrep=ab_irrep)


def reference(amplitudes, integrals, pair_irrep, cd_irrep, ab_irrep):
    def per_block(pieces):
        block_amps, block_labels = pieces
        symmetric = jnp.where(block_labels[:, None] == cd_irrep[None, :], block_amps, jnp.zeros_like(block_amps))
        summed = lax.dot_general(symmetric, integrals, (((1,), (1,)), ((), ())), preferred_element_type=jnp.float32)
        kept = jnp.where(block_labels[:, None] == ab_irrep[None, :], summed, jnp.zeros_like(summed))
        return kept.astype(jnp.bfloat16)

    return lax.map(per_block, (amplitudes, pair_irrep))
```

```python
import jax
import jax.numpy as jnp
from jax import lax
from jax.experimental import pallas as pl
from jax.experimental.pallas import tpu as pltpu
from jax.sharding import Mesh, PartitionSpec as P

X, Z, CORES, Y = 4, 16, 2, 4
ROWS = 4
OWN = 9
CDS = 256
AB = X * Z * CORES * OWN
LABELLED = AB + 16
CUT = 576
GROUP = Z * CORES * ROWS
BF, F32 = jnp.bfloat16, jnp.float32
VMEM = pl.BlockSpec(memory_space=pltpu.VMEM)


def prepare_kernel(amps, integrals, labels, sent, labelled):
    for x in range(X):
        for zc in range(Z * CORES):
            start = (x * Z * CORES + zc) * CDS
            sent[zc, :, x * CDS:(x + 1) * CDS] = amps[0, :, start:start + CDS]
    labelled[:AB] = integrals[...]
    row = labels[...].astype(F32)
    labelled[AB:] = jnp.broadcast_to(row, (16, CDS)).astype(BF)


def multiply_kernel(place, amps, rows, own, left, right, far_top, far_bottom, mine, other, stacked, acc):
    x, core = place[0], place[1]
    for zc in range(Z * CORES):
        block = amps[zc].astype(F32)
        for k in range(X):
            stacked[k, zc * ROWS:(zc + 1) * ROWS, :] = block[:, k * CDS:(k + 1) * CDS]
    row_labels = rows[...]

    def masked(k, labels):
        values = stacked[k]
        labels = labels.astype(F32)[:1]
        return jnp.where(row_labels == labels, values, jnp.zeros_like(values)).astype(BF)

    def times(block, values):
        return lax.dot_general(block, values, (((1,), (1,)), ((), ())), preferred_element_type=F32)

    a_own = masked(x, own[AB:])
    a_left = masked(lax.rem(x + X - 1, X), left[AB:])
    a_right = masked(lax.rem(x + 1, X), right[AB:])
    a_far = masked(lax.rem(x + 2, X), far_bottom[AB - CUT:])
    step = 192
    for start in range(0, AB, step):
        part = pl.ds(start, step)
        far = far_top[part] if start < CUT else far_bottom[pl.ds(start - CUT, step)]
        acc[part] = (times(own[part], a_own) + times(left[part], a_left)) + (
            times(right[part], a_right) + times(far, a_far))
    first = core == 0
    for z in range(Z):
        for k in range(X):
            start = (k * Z + z) * CORES * OWN
            low, high = acc[start:start + OWN], acc[start + OWN:start + 2 * OWN]
            mine[z, k * OWN:(k + 1) * OWN, :] = jnp.where(first, low, high)
            other[z, k * OWN:(k + 1) * OWN, :] = jnp.where(first, high, low)


def sum_kernel(partials, out, total):
    value = partials[0].astype(F32)
    for z in range(1, Z):
        value = value + partials[z].astype(F32)
    total[...] = value
    for k in range(X):
        out[k] = total[k * OWN:(k + 1) * OWN, :].astype(BF)


def finish_kernel(parts, rows, abs_, out):
    for k in range(X):
        lanes = slice(k * GROUP, (k + 1) * GROUP)
        value = parts[k].astype(F32)
        keep = rows[:, lanes] == abs_[...]
        out[:, lanes] = jnp.where(keep, value, jnp.zeros_like(value)).astype(BF)


def call(kernel, out_shape, scratch=(), specs=None, n=0):
    return pl.pallas_call(
        kernel,
        out_shape=out_shape,
        in_specs=[pl.BlockSpec(memory_space=pltpu.SMEM)] * n + [VMEM] * (specs - n),
        out_specs=jax.tree.map(lambda _: VMEM, out_shape),
        scratch_shapes=list(scratch),
        compiler_params=pltpu.CompilerParams(vmem_limit_bytes=40 * 2**20),
    )


def body(amplitudes, integrals, pair_irrep, cd_irrep, ab_irrep):
    shape = jax.ShapeDtypeStruct
    x, core = lax.axis_index("x"), lax.axis_index("core")
    sent, labelled = call(
        prepare_kernel,
        (shape((Z * CORES, ROWS, X * CDS), BF), shape((LABELLED, CDS), BF)),
        specs=3,
    )(amplitudes, integrals, cd_irrep[None])
    up = [(i, (i + 1) % X) for i in range(X)]
    down = [(i, (i - 1) % X) for i in range(X)]
    left = lax.ppermute(labelled, "x", up)
    right = lax.ppermute(labelled, "x", down)
    amps = lax.all_to_all(sent, ("z", "core"), 0, 0, tiled=True)
    far_top = lax.ppermute(left[:CUT], "x", up)
    far_bottom = lax.ppermute(right[CUT:], "x", down)
    rows = lax.dynamic_slice_in_dim(pair_irrep.reshape(X, GROUP), x, 1, 0)
    rows = rows.reshape(GROUP, 1).astype(F32)
    place = jnp.stack([x, core]).astype(jnp.int32)
    sums = shape((Z, X * OWN, GROUP), F32)
    mine, other = call(
        multiply_kernel,
        (sums, sums),
        scratch=[pltpu.VMEM((X, GROUP, CDS), F32), pltpu.VMEM((AB, GROUP), F32)],
        specs=8, n=1,
    )(place, amps, rows, labelled, left, right, far_top, far_bottom)
    theirs = lax.ppermute(other, "core", [(0, 1), (1, 0)])
    partials = (mine + theirs).astype(BF)
    partials = lax.all_to_all(partials, "z", 0, 0, tiled=True)
    parts = call(
        sum_kernel, shape((X, OWN, GROUP), BF), scratch=[pltpu.VMEM((X * OWN, GROUP), F32)], specs=1
    )(partials)
    parts = lax.all_to_all(parts, "x", 0, 0, tiled=True)
    out = call(finish_kernel, shape((OWN, X * GROUP), BF), specs=3)(parts, pair_irrep, ab_irrep[:, None])
    return out.T[None]


def solution(mesh):
    split = Mesh(mesh.devices.reshape(X, Z, CORES, Y), ("x", "z", "core", "y"))
    cd = ("x", "z", "core")
    placed = (P("y", cd, None), P(None, cd), P("y", None), P(cd), P(cd))
    return jax.shard_map(body, mesh=split, in_specs=placed, out_specs=P("y", None, cd), check_vma=False)
```

```python
import jax
import jax.numpy as jnp
from jax import lax
from jax.experimental import pallas as pl
from jax.experimental.pallas import tpu as pltpu
from jax.sharding import Mesh, PartitionSpec as P

X, Z, CORES, Y = 4, 16, 2, 4
ROWS = 4
OWN = 9
CDS = 256
PART = Z * CORES * OWN
TALL = PART + 16
WIDE = CORES * CDS
LINE = Z * ROWS
BF, F32 = jnp.bfloat16, jnp.float32
HBM = pl.BlockSpec(memory_space=pltpu.HBM)
VMEM = pl.BlockSpec(memory_space=pltpu.VMEM)
SMEM = pl.BlockSpec(memory_space=pltpu.SMEM)


def regroup_kernel(amps, sent, amps_in, sem):
    load = pltpu.make_async_copy(amps.at[0], amps_in, sem)
    load.start()
    load.wait()
    for x in range(X):
        for z in range(Z):
            start = (x * Z + z) * WIDE
            sent[z, :, x * WIDE:(x + 1) * WIDE] = amps_in[:, start:start + WIDE]


def slice_kernel(place, integrals, labels, *outs):
    row = jnp.broadcast_to(labels[...].astype(F32), (TALL - PART, CDS)).astype(BF)
    for step, out in enumerate(outs):
        start = lax.rem(place[0] + step, X) * PART
        out[:PART] = integrals[pl.ds(pl.multiple_of(start, 32), PART), :]
        out[PART:] = row


def stack_kernel(*refs):
    out = refs[-1]
    for step, ref in enumerate(refs[:-1]):
        out[step] = ref[...]


def multiply_kernel(place, *refs):
    amps, (rows, mine, other, out, stacked, acc) = refs[:X], refs[X:]
    x, first = place[0], place[1] == 0
    for step in range(X):
        source = lax.rem(x + X - step, X)
        for z in range(Z):
            stacked[source, z * ROWS:(z + 1) * ROWS, :] = amps[step][z].astype(F32)
    row_labels = rows[...]
    total = jnp.zeros((PART, X * LINE), F32)
    for step in range(X):
        source = lax.rem(x + X - step, X)
        lanes = pl.ds(pl.multiple_of(source * WIDE, WIDE), WIDE)
        values = jnp.concatenate([stacked[k, :, lanes] for k in range(X)], axis=0)
        halves = values[:, :CDS], values[:, CDS:]
        pairs = (
            (mine, jnp.where(first, halves[0], halves[1])),
            (other, jnp.where(first, halves[1], halves[0])),
        )
        for blocks, half in pairs:
            labels = blocks[step, PART:].astype(F32)[:1]
            kept = jnp.where(row_labels == labels, half, jnp.zeros_like(half)).astype(BF)
            total += lax.dot_general(
                blocks[step, :PART], kept, (((1,), (1,)), ((), ())), preferred_element_type=F32
            )
    acc[...] = total
    for z in range(Z):
        out[z] = acc[z * CORES * OWN:(z + 1) * CORES * OWN, :].astype(BF)


def sum_kernel(place, partials, own, sent, total):
    core = place[1]
    value = partials[0].astype(F32)
    for z in range(1, Z):
        value = value + partials[z].astype(F32)
    value = value.astype(BF)
    pairs = 2 * LINE
    i = lax.broadcasted_iota(jnp.int32, (pairs, CORES * pairs), 0)
    j = lax.broadcasted_iota(jnp.int32, (pairs, CORES * pairs), 1)
    goal = (i // ROWS) * (CORES * ROWS) + core * ROWS + lax.rem(i, ROWS)
    spread = jnp.where(j == goal, 1.0, 0.0).astype(BF)
    for k in range(X // 2):
        total[:, k * CORES * pairs:(k + 1) * CORES * pairs] = jnp.dot(
            value[:, k * pairs:(k + 1) * pairs], spread, preferred_element_type=F32
        )
    low, high = total[:OWN, :], total[OWN:, :]
    own[...] = jnp.where(core == 0, low, high).astype(BF)
    sent[...] = jnp.where(core == 0, high, low).astype(BF)


def finish_kernel(own, got, rows, abs_, out):
    value = own[...].astype(F32) + got[...].astype(F32)
    keep = rows[...] == abs_[...]
    out[...] = jnp.where(keep, value, jnp.zeros_like(value)).astype(BF)


def call(kernel, out_shape, in_specs, scratch=()):
    return pl.pallas_call(
        kernel,
        out_shape=out_shape,
        in_specs=in_specs,
        out_specs=jax.tree.map(lambda _: VMEM, out_shape),
        scratch_shapes=list(scratch),
        compiler_params=pltpu.CompilerParams(vmem_limit_bytes=32 * 2**20),
    )


def along_x(value, step):
    return lax.ppermute(value, "x", [(i, (i + step) % X) for i in range(X)])


def body(amplitudes, integrals, pair_irrep, cd_irrep, ab_irrep):
    shape = jax.ShapeDtypeStruct
    core = lax.axis_index("core")
    swap = [(0, 1), (1, 0)]
    place = jnp.stack([lax.axis_index("x"), core]).astype(jnp.int32)
    sent = call(
        regroup_kernel, shape((Z, ROWS, X * WIDE), BF), [HBM],
        [pltpu.VMEM((ROWS, X * Z * WIDE), BF), pltpu.SemaphoreType.DMA],
    )(amplitudes)
    amps = lax.all_to_all(sent, "z", 0, 0, tiled=True)
    slices = call(slice_kernel, (shape((TALL, CDS), BF),) * X, [SMEM, VMEM, VMEM])(place, integrals, cd_irrep[None])
    gathered = [slices[0]] + [along_x(slices[step], step) for step in range(1, X)]
    mine = call(stack_kernel, shape((X, TALL, CDS), BF), [VMEM] * X)(*gathered)
    other = lax.ppermute(mine, "core", swap)
    rows = lax.dynamic_slice_in_dim(pair_irrep.reshape(X * Z, CORES, ROWS), core, 1, 1)
    rows = rows.reshape(X * LINE, 1).astype(F32)
    all_amps = [amps] + [along_x(amps, step) for step in range(1, X)]
    partials = call(
        multiply_kernel, shape((Z, CORES * OWN, X * LINE), BF), [SMEM] + [VMEM] * (X + 3),
        [pltpu.VMEM((X, LINE, X * WIDE), F32), pltpu.VMEM((PART, X * LINE), F32)],
    )(place, *all_amps, rows, mine, other)
    partials = lax.all_to_all(partials, "z", 0, 0, tiled=True)
    final = shape((OWN, X * CORES * LINE), BF)
    own, away = call(
        sum_kernel, (final, final), [SMEM, VMEM], [pltpu.VMEM((CORES * OWN, X * CORES * LINE), F32)]
    )(place, partials)
    got = lax.ppermute(away, "core", swap)
    out = call(finish_kernel, final, [VMEM] * 4)(own, got, pair_irrep, ab_irrep[:, None])
    return out.T[None]


def solution(mesh):
    split = Mesh(mesh.devices.reshape(X, Z, CORES, Y), ("x", "z", "core", "y"))
    cd = ("x", "z", "core")
    placed = (P("y", cd, None), P(None, cd), P("y", None), P(cd), P(cd))
    return jax.shard_map(body, mesh=split, in_specs=placed, out_specs=P("y", None, cd), check_vma=False)
```

```python
import jax
import jax.numpy as jnp
from jax import lax
from jax.experimental import pallas as pl
from jax.experimental.pallas import tpu as pltpu
from jax.sharding import Mesh, PartitionSpec as P

X, Z, CORES, Y = 4, 16, 2, 4
ROWS = 4
OWN = 9
CDS = 256
AB = X * Z * CORES * OWN
TALL = AB + 16
WIDE = CORES * CDS
LINE = Z * ROWS
HELD = X // 2 * CORES * OWN
BF, F32 = jnp.bfloat16, jnp.float32
HBM = pl.BlockSpec(memory_space=pltpu.HBM)
VMEM = pl.BlockSpec(memory_space=pltpu.VMEM)
SMEM = pl.BlockSpec(memory_space=pltpu.SMEM)


def label_kernel(integrals, labels, labelled):
    labelled[:AB] = integrals[...]
    labelled[AB:] = jnp.broadcast_to(labels[...].astype(F32), (TALL - AB, CDS)).astype(BF)


def regroup_kernel(amps, after, sent):
    for x in range(X):
        for z in range(Z):
            start = (x * Z + z) * WIDE
            sent[z, :, x * WIDE:(x + 1) * WIDE] = amps[0, :, start:start + WIDE]


def multiply_kernel(place, amps, rows, *refs):
    blocks, (out, stacked, acc) = refs[:X * CORES], refs[X * CORES:]
    x, core = place[0], place[1]
    for z in range(Z):
        stacked[z * ROWS:(z + 1) * ROWS, :] = amps[z].astype(F32)
    row_labels = rows[...]
    kept = []
    for c in range(CORES):
        for step in range(X):
            source = lax.rem(x + X - step, X) * CORES + (core if c == 0 else 1 - core)
            values = stacked[:, pl.ds(pl.multiple_of(source * CDS, CDS), CDS)]
            labels = blocks[c * X + step][AB:].astype(F32)[:1]
            kept.append(jnp.where(row_labels == labels, values, jnp.zeros_like(values)).astype(BF))
    tile = 192
    for start in range(0, AB // 2, tile):
        halves = []
        for base in (start, start + AB // 2):
            total = None
            for block, value in zip(blocks, kept):
                term = lax.dot_general(
                    block[base:base + tile], value, (((1,), (1,)), ((), ())), preferred_element_type=F32
                )
                total = term if total is None else total + term
            halves.append(total)
        acc[start:start + tile] = jnp.concatenate(halves, axis=1)
    pairs = CORES * OWN
    for z in range(Z):
        parts = [acc[(k * Z + z) * pairs:(k * Z + z + 1) * pairs, :] for k in range(X // 2)]
        out[z] = jnp.concatenate(parts, axis=0).astype(BF)


def sum_kernel(place, partials, out, total):
    core = place[1]
    value = partials[0].astype(F32)
    for z in range(1, Z):
        value = value + partials[z].astype(F32)
    value = value.astype(BF)
    i = lax.broadcasted_iota(jnp.int32, (2 * LINE, CORES * LINE), 0)
    j = lax.broadcasted_iota(jnp.int32, (2 * LINE, CORES * LINE), 1)
    for half in range(2):
        pair = i - half * LINE
        goal = (pair // ROWS) * (CORES * ROWS) + core * ROWS + lax.rem(i, ROWS)
        spread = jnp.where((j == goal) & (pair >= 0) & (pair < LINE), 1.0, 0.0).astype(BF)
        total[half] = jnp.dot(value, spread, preferred_element_type=F32)
    for k in range(X):
        for c in range(CORES):
            start = (k % 2 * CORES + c) * OWN
            out[k * CORES + c] = total[k // 2, start:start + OWN, :].astype(BF)


def finish_kernel(parts, rows, abs_, out):
    width = CORES * LINE
    for k in range(X):
        lanes = slice(k * width, (k + 1) * width)
        value = parts[k * CORES].astype(F32) + parts[k * CORES + 1].astype(F32)
        keep = rows[:, lanes] == abs_[...]
        out[:, lanes] = jnp.where(keep, value, jnp.zeros_like(value)).astype(BF)


def call(kernel, out_shape, in_specs, scratch=(), cost=None):
    if cost:
        cost = pl.CostEstimate(flops=cost, bytes_accessed=0, transcendentals=0)
    return pl.pallas_call(
        kernel,
        out_shape=out_shape,
        in_specs=in_specs,
        out_specs=jax.tree.map(lambda _: VMEM, out_shape),
        scratch_shapes=list(scratch),
        cost_estimate=cost,
        compiler_params=pltpu.CompilerParams(vmem_limit_bytes=32 * 2**20),
    )


def along_x(value, step):
    return lax.ppermute(value, "x", [(i, (i + step) % X) for i in range(X)])


def body(amplitudes, integrals, pair_irrep, cd_irrep, ab_irrep):
    shape = jax.ShapeDtypeStruct
    core = lax.axis_index("core")
    swap = [(0, 1), (1, 0)]
    place = jnp.stack([lax.axis_index("x"), core]).astype(jnp.int32)
    labelled = call(label_kernel, shape((TALL, CDS), BF), [VMEM, VMEM])(integrals, cd_irrep[None])
    gathered = [labelled] + [along_x(labelled, step) for step in (1, 2, 3)]
    sent = call(
        regroup_kernel, shape((Z, ROWS, X * WIDE), BF), [VMEM, pl.BlockSpec(memory_space=pl.ANY)], cost=None
    )(amplitudes, labelled)
    amps = lax.all_to_all(sent, "z", 0, 0, tiled=True)
    gathered += [lax.ppermute(value, "core", swap) for value in gathered]
    rows = lax.dynamic_slice_in_dim(pair_irrep.reshape(X * Z, CORES, ROWS), lax.axis_index("x") * Z, Z, 0)
    rows = lax.dynamic_slice_in_dim(rows, core, 1, 1)
    rows = rows.reshape(LINE, 1).astype(F32)
    partials = call(
        multiply_kernel, shape((Z, HELD, 2 * LINE), BF), [SMEM] + [VMEM] * (2 + X * CORES),
        [pltpu.VMEM((LINE, X * WIDE), F32), pltpu.VMEM((AB // 2, 2 * LINE), F32)],
    )(place, amps, rows, *gathered)
    partials = lax.all_to_all(partials, "z", 0, 0, tiled=True)
    parts = call(
        sum_kernel, shape((X * CORES, OWN, CORES * LINE), BF), [SMEM, VMEM],
        [pltpu.VMEM((2, HELD, CORES * LINE), F32)],
    )(place, partials)
    parts = lax.all_to_all(parts, ("x", "core"), 0, 0, tiled=True)
    final = shape((OWN, X * CORES * LINE), BF)
    out = call(finish_kernel, final, [VMEM] * 3)(parts, pair_irrep, ab_irrep[:, None])
    return out.T[None]


def solution(mesh):
    split = Mesh(mesh.devices.reshape(X, Z, CORES, Y), ("x", "z", "core", "y"))
    cd = ("x", "z", "core")
    placed = (P("y", cd, None), P(None, cd), P("y", None), P(cd), P(cd))
    return jax.shard_map(body, mesh=split, in_specs=placed, out_specs=P("y", None, cd), check_vma=False)
```

```python
import jax
import jax.numpy as jnp
from jax import lax
from jax.experimental import pallas as pl
from jax.experimental.pallas import tpu as pltpu
from jax.sharding import Mesh, PartitionSpec as P

X, Z, CORES, Y = 4, 16, 2, 4
ROWS = 4
OWN = 9
CDS = 256
AB = X * Z * CORES * OWN
TALL = AB + 16
WIDE = CORES * CDS
LINE = Z * ROWS
HELD = X // 2 * CORES * OWN
BF, F32 = jnp.bfloat16, jnp.float32
HBM = pl.BlockSpec(memory_space=pltpu.HBM)
VMEM = pl.BlockSpec(memory_space=pltpu.VMEM)
SMEM = pl.BlockSpec(memory_space=pltpu.SMEM)


def regroup_kernel(amps, after, sent):
    for x in range(X):
        for z in range(Z):
            start = (x * Z + z) * WIDE
            sent[z, :, x * WIDE:(x + 1) * WIDE] = amps[0, :, start:start + WIDE]


def multiply_kernel(place, amps, rows, *refs):
    blocks, (out, stacked, acc) = refs[:X * CORES], refs[X * CORES:]
    x, core = place[0], place[1]
    for z in range(Z):
        stacked[z * ROWS:(z + 1) * ROWS, :] = amps[z].astype(F32)
    row_labels = rows[...]
    kept = []
    for c in range(CORES):
        for step in range(X):
            source = lax.rem(x + X - (0, 2, 1, 3)[step], X) * CORES + (core if c == 0 else 1 - core)
            values = stacked[:, pl.ds(pl.multiple_of(source * CDS, CDS), CDS)]
            labels = blocks[c * X + step][AB:].astype(F32)[:1]
            kept.append(jnp.where(row_labels == labels, values, jnp.zeros_like(values)).astype(BF))
    tile = 192
    for start in range(0, AB // 2, tile):
        halves = []
        for base in (start, start + AB // 2):
            total = None
            for block, value in zip(blocks, kept):
                term = lax.dot_general(
                    block[base:base + tile], value, (((1,), (1,)), ((), ())), preferred_element_type=F32
                )
                total = term if total is None else total + term
            halves.append(total)
        acc[start:start + tile] = jnp.concatenate(halves, axis=1)
    pairs = CORES * OWN
    for z in range(Z):
        parts = [acc[(k * Z + z) * pairs:(k * Z + z + 1) * pairs, :] for k in range(X // 2)]
        out[z] = jnp.concatenate(parts, axis=0).astype(BF)


def sum_kernel(place, partials, out, total):
    core = place[1]
    value = partials[0].astype(F32)
    for z in range(1, Z):
        value = value + partials[z].astype(F32)
    value = value.astype(BF)
    i = lax.broadcasted_iota(jnp.int32, (2 * LINE, CORES * LINE), 0)
    j = lax.broadcasted_iota(jnp.int32, (2 * LINE, CORES * LINE), 1)
    for half in range(2):
        pair = i - half * LINE
        goal = (pair // ROWS) * (CORES * ROWS) + core * ROWS + lax.rem(i, ROWS)
        spread = jnp.where((j == goal) & (pair >= 0) & (pair < LINE), 1.0, 0.0).astype(BF)
        total[half] = jnp.dot(value, spread, preferred_element_type=F32)
    for k in range(X):
        for c in range(CORES):
            start = (k % 2 * CORES + c) * OWN
            out[k * CORES + c] = total[k // 2, start:start + OWN, :].astype(BF)


def finish_kernel(parts, rows, abs_, out):
    width = CORES * LINE
    for k in range(X):
        lanes = slice(k * width, (k + 1) * width)
        value = parts[k * CORES].astype(F32) + parts[k * CORES + 1].astype(F32)
        keep = rows[:, lanes] == abs_[...]
        out[:, lanes] = jnp.where(keep, value, jnp.zeros_like(value)).astype(BF)


def call(kernel, out_shape, in_specs, scratch=(), cost=None):
    if cost:
        cost = pl.CostEstimate(flops=cost, bytes_accessed=0, transcendentals=0)
    return pl.pallas_call(
        kernel,
        out_shape=out_shape,
        in_specs=in_specs,
        out_specs=jax.tree.map(lambda _: VMEM, out_shape),
        scratch_shapes=list(scratch),
        cost_estimate=cost,
        compiler_params=pltpu.CompilerParams(vmem_limit_bytes=32 * 2**20),
    )


def along_x(value, step):
    return lax.ppermute(value, "x", [(i, (i + step) % X) for i in range(X)])


def body(amplitudes, integrals, pair_irrep, cd_irrep, ab_irrep):
    shape = jax.ShapeDtypeStruct
    core = lax.axis_index("core")
    swap = [(0, 1), (1, 0)]
    place = jnp.stack([lax.axis_index("x"), core]).astype(jnp.int32)
    irreps = jnp.broadcast_to(cd_irrep[None].astype(BF), (TALL - AB, CDS))
    labelled = jnp.concatenate([integrals, irreps], axis=0)
    gathered = [labelled] + [along_x(labelled, step) for step in (2, 1, 3)]
    sent = call(
        regroup_kernel, shape((Z, ROWS, X * WIDE), BF), [VMEM, pl.BlockSpec(memory_space=pl.ANY)], cost=None
    )(amplitudes, labelled)
    amps = lax.all_to_all(sent, "z", 0, 0, tiled=True)
    gathered += [lax.ppermute(value, "core", swap) for value in gathered]
    rows = lax.dynamic_slice_in_dim(pair_irrep.reshape(X * Z, CORES, ROWS), lax.axis_index("x") * Z, Z, 0)
    rows = lax.dynamic_slice_in_dim(rows, core, 1, 1)
    rows = rows.reshape(LINE, 1).astype(F32)
    partials = call(
        multiply_kernel, shape((Z, HELD, 2 * LINE), BF), [SMEM] + [VMEM] * (2 + X * CORES),
        [pltpu.VMEM((LINE, X * WIDE), F32), pltpu.VMEM((AB // 2, 2 * LINE), F32)],
    )(place, amps, rows, *gathered)
    partials = lax.all_to_all(partials, "z", 0, 0, tiled=True)
    parts = call(
        sum_kernel, shape((X * CORES, OWN, CORES * LINE), BF), [SMEM, VMEM],
        [pltpu.VMEM((2, HELD, CORES * LINE), F32)],
    )(place, partials)
    parts = lax.all_to_all(parts, ("x", "core"), 0, 0, tiled=True)
    final = shape((OWN, X * CORES * LINE), BF)
    out = call(finish_kernel, final, [VMEM] * 3)(parts, pair_irrep, ab_irrep[:, None])
    return out.T[None]


def solution(mesh):
    split = Mesh(mesh.devices.reshape(X, Z, CORES, Y), ("x", "z", "core", "y"))
    cd = ("x", "z", "core")
    placed = (P("y", cd, None), P(None, cd), P("y", None), P(cd), P(cd))
    return jax.shard_map(body, mesh=split, in_specs=placed, out_specs=P("y", None, cd), check_vma=False)
```

```python
import jax
import jax.numpy as jnp
from jax import lax
from jax.experimental import pallas as pl
from jax.experimental.pallas import tpu as pltpu
from jax.sharding import Mesh, PartitionSpec as P

X, Z, CORES, Y = 4, 16, 2, 4
ROWS = 4
OWN = 9
CDS = 256
AB = X * Z * CORES * OWN
TALL = AB + 16
WIDE = CORES * CDS
LINE = Z * ROWS
HELD = X // 2 * CORES * OWN
BF, F32 = jnp.bfloat16, jnp.float32
HBM = pl.BlockSpec(memory_space=pltpu.HBM)
VMEM = pl.BlockSpec(memory_space=pltpu.VMEM)
SMEM = pl.BlockSpec(memory_space=pltpu.SMEM)


def regroup_kernel(amps, after, sent):
    for x in range(X):
        for z in range(Z):
            start = (x * Z + z) * WIDE
            sent[z, :, x * WIDE:(x + 1) * WIDE] = amps[0, :, start:start + WIDE]


def multiply_kernel(place, amps, rows, *refs):
    blocks, (out, stacked, acc) = refs[:X * CORES], refs[X * CORES:]
    x, core = place[0], place[1]
    for z in range(Z):
        stacked[z * ROWS:(z + 1) * ROWS, :] = amps[z].astype(F32)
    row_labels = rows[...]
    kept = []
    for c in range(CORES):
        for step in range(X):
            source = lax.rem(x + X - (0, 2, 1, 3)[step], X) * CORES + (core if c == 0 else 1 - core)
            values = stacked[:, pl.ds(pl.multiple_of(source * CDS, CDS), CDS)]
            labels = blocks[c * X + step][AB:].astype(F32)[:1]
            kept.append(jnp.where(row_labels == labels, values, jnp.zeros_like(values)).astype(BF))
    kept = jnp.concatenate(kept, axis=1)
    tile = 192
    for start in range(0, AB // 2, tile):
        halves = []
        for base in (start, start + AB // 2):
            part = jnp.concatenate([block[base:base + tile] for block in blocks], axis=1)
            halves.append(lax.dot_general(part, kept, (((1,), (1,)), ((), ())), preferred_element_type=F32))
        acc[start:start + tile] = jnp.concatenate(halves, axis=1)
    pairs = CORES * OWN
    for z in range(Z):
        parts = [acc[(k * Z + z) * pairs:(k * Z + z + 1) * pairs, :] for k in range(X // 2)]
        out[z] = jnp.concatenate(parts, axis=0).astype(BF)


def sum_kernel(place, partials, out, total):
    core = place[1]
    value = partials[0].astype(F32)
    for z in range(1, Z):
        value = value + partials[z].astype(F32)
    value = value.astype(BF)
    i = lax.broadcasted_iota(jnp.int32, (2 * LINE, CORES * LINE), 0)
    j = lax.broadcasted_iota(jnp.int32, (2 * LINE, CORES * LINE), 1)
    for half in range(2):
        pair = i - half * LINE
        goal = (pair // ROWS) * (CORES * ROWS) + core * ROWS + lax.rem(i, ROWS)
        spread = jnp.where((j == goal) & (pair >= 0) & (pair < LINE), 1.0, 0.0).astype(BF)
        total[half] = jnp.dot(value, spread, preferred_element_type=F32)
    for k in range(X):
        for c in range(CORES):
            start = (k % 2 * CORES + c) * OWN
            out[k * CORES + c] = total[k // 2, start:start + OWN, :].astype(BF)


def finish_kernel(parts, rows, abs_, out):
    width = CORES * LINE
    for k in range(X):
        lanes = slice(k * width, (k + 1) * width)
        value = parts[k * CORES].astype(F32) + parts[k * CORES + 1].astype(F32)
        keep = rows[:, lanes] == abs_[...]
        out[:, lanes] = jnp.where(keep, value, jnp.zeros_like(value)).astype(BF)


def call(kernel, out_shape, in_specs, scratch=(), cost=None):
    if cost:
        cost = pl.CostEstimate(flops=cost, bytes_accessed=0, transcendentals=0)
    return pl.pallas_call(
        kernel,
        out_shape=out_shape,
        in_specs=in_specs,
        out_specs=jax.tree.map(lambda _: VMEM, out_shape),
        scratch_shapes=list(scratch),
        cost_estimate=cost,
        compiler_params=pltpu.CompilerParams(vmem_limit_bytes=32 * 2**20),
    )


def along_x(value, step):
    return lax.ppermute(value, "x", [(i, (i + step) % X) for i in range(X)])


def body(amplitudes, integrals, pair_irrep, cd_irrep, ab_irrep):
    shape = jax.ShapeDtypeStruct
    core = lax.axis_index("core")
    swap = [(0, 1), (1, 0)]
    place = jnp.stack([lax.axis_index("x"), core]).astype(jnp.int32)
    irreps = jnp.broadcast_to(cd_irrep[None].astype(BF), (TALL - AB, CDS))
    labelled = jnp.concatenate([integrals, irreps], axis=0)
    gathered = [labelled] + [along_x(labelled, step) for step in (2, 1, 3)]
    sent = call(
        regroup_kernel, shape((Z, ROWS, X * WIDE), BF), [VMEM, pl.BlockSpec(memory_space=pl.ANY)], cost=None
    )(amplitudes, labelled)
    amps = lax.all_to_all(sent, "z", 0, 0, tiled=True)
    gathered += [lax.ppermute(value, "core", swap) for value in gathered]
    rows = lax.dynamic_slice_in_dim(pair_irrep.reshape(X * Z, CORES, ROWS), lax.axis_index("x") * Z, Z, 0)
    rows = lax.dynamic_slice_in_dim(rows, core, 1, 1)
    rows = rows.reshape(LINE, 1).astype(F32)
    partials = call(
        multiply_kernel, shape((Z, HELD, 2 * LINE), BF), [SMEM] + [VMEM] * (2 + X * CORES),
        [pltpu.VMEM((LINE, X * WIDE), F32), pltpu.VMEM((AB // 2, 2 * LINE), F32)],
    )(place, amps, rows, *gathered)
    partials = lax.all_to_all(partials, "z", 0, 0, tiled=True)
    parts = call(
        sum_kernel, shape((X * CORES, OWN, CORES * LINE), BF), [SMEM, VMEM],
        [pltpu.VMEM((2, HELD, CORES * LINE), F32)],
    )(place, partials)
    parts = lax.all_to_all(parts, ("x", "core"), 0, 0, tiled=True)
    final = shape((OWN, X * CORES * LINE), BF)
    out = call(finish_kernel, final, [VMEM] * 3)(parts, pair_irrep, ab_irrep[:, None])
    return out.T[None]


def solution(mesh):
    split = Mesh(mesh.devices.reshape(X, Z, CORES, Y), ("x", "z", "core", "y"))
    cd = ("x", "z", "core")
    placed = (P("y", cd, None), P(None, cd), P("y", None), P(cd), P(cd))
    return jax.shard_map(body, mesh=split, in_specs=placed, out_specs=P("y", None, cd), check_vma=False)
```
